32 devices in a mesh: rep: 4 (over z), fsdp: 8 (over y, x, core).
Axes of the slice: x: 2, y: 2, z: 4, core: 2. Of those that a mesh axis runs over, the one named last changes fastest.
Arguments:
- tokens: bfloat16 [8192, 4096], P(('rep', 'fsdp')), may hold values from -6 to 6
- out_grad: bfloat16 [8192, 14336], P(('rep', 'fsdp')), may hold values from -6 to 6
- weight_blocks: bfloat16 [64, 128, 128], P('fsdp'), may hold values from -0.375 to 0.375
- block_row: int32 [64], replicated, may hold values from 0 to 31, as said below
- block_col: int32 [64], replicated, may hold values from 0 to 111
- send_list: int32 [8, 4, 3], P('fsdp'), may hold values from 0 to 8, as said below
Outputs:
- token_grad: bfloat16 [8192, 4096], P(('rep', 'fsdp'))
- grad_owned: float32 [4, 8, 3, 128, 128], P('rep', 'fsdp')
The draws below stay inside these ranges and needn't reach their ends.
Inputs may be any that keep to these rules, and one draw needn't show every extreme that they name: The pairs (block_row[k], block_col[k]) are all distinct. For each f, every local block number 0 to 7 stands exactly once in send_list[f] over all owners and slots, in increasing order within an owner's slots, followed by the pad value 8; for each f some owner fills all 3 slots.
All inputs are finite; a program needn't handle non-finite values.
Results may differ from the reference program's by a relative error of at most 0.001.
Values may be sent and summed in bfloat16 or wider, within the bound.
A program may use at most 256 MiB of HBM per device.

```python
import jax
import jax.numpy as jnp
from jax import lax

D = 4096
FF = 14336
BS = 128
BLK_DEV = 8
CAP = 3
TOKENS = 8192
NNZ = 64
N_REP = 4
N_FSDP = 8


def pattern(key):
    base_key = jax.random.fold_in(key, 7)
    first_key, second_key = jax.random.split(base_key)
    row_total = D // BS
    col_total = FF // BS
    serial = jnp.arange(NNZ, dtype=jnp.int32)
    shifts = jax.random.randint(first_key, (row_total,), 0, col_total).astype(jnp.int32)
    shifts = shifts.at[0].set(col_total - 1)
    row_raw = serial % row_total
    col_raw = (serial // row_total + shifts[row_raw]) % col_total
    shuffle = jax.random.permutation(second_key, NNZ)
    return (row_raw[shuffle].astype(jnp.int32), col_raw[shuffle].astype(jnp.int32))


def draw_block_row(key, part):
    return pattern(key)[0]


def draw_block_col(key, part):
    return pattern(key)[1]


def draw_send_list(key, part):

    def one_shard(shard_key):
        first_key, second_key = jax.random.split(shard_key)
        busiest = jax.random.randint(first_key, (), 0, N_REP).astype(jnp.int32)
        position = jax.random.permutation(second_key, BLK_DEV).astype(jnp.int32)
        others = (busiest + 1 + (position - CAP) % (N_REP - 1)) % N_REP
        owners = jnp.where(position < CAP, busiest, others).astype(jnp.int32)
        peers = jnp.arange(N_REP, dtype=jnp.int32)
        local_ids = jnp.arange(BLK_DEV, dtype=jnp.int32)
        sort_keys = (owners[None, :] != peers[:, None]).astype(jnp.int32) * BLK_DEV + local_ids[None, :]
        ranked = jnp.argsort(sort_keys, axis=1)[:, :CAP].astype(jnp.int32)
        matches = owners[ranked] == peers[:, None]
        return jnp.where(matches, ranked, BLK_DEV).astype(jnp.int32)
    shard_keys = jax.random.split(jax.random.fold_in(key, 11), N_FSDP)
    return jax.vmap(one_shard)(shard_keys)


def level_of(own_key, shape, cuts, smallest, top_value):
    factor_of, own = 1.0, jax.random.fold_in(own_key, 6)
    for dim, parts in cuts:
        steps = jnp.exp(jax.random.uniform(jax.random.fold_in(own, dim), (parts,), jnp.float32, smallest / len(cuts), top_value / len(cuts)))
        factor_of = factor_of * jnp.repeat(steps, shape[dim] // parts).reshape([-1 if axis == dim else 1 for axis in range(len(shape))])
    return factor_of


def bell_draw(stream_key, extent, width, bound, shards=(), kind=jnp.bfloat16):
    result = jax.random.normal(stream_key, extent, jnp.float32) * width
    if len(shards) > 0:
        result = level_of(stream_key, extent, shards, -0.22, 0.18) * result
    return jnp.clip(result, min=-bound, max=bound).astype(kind)


def setup_inputs(seed: int = 0) -> dict:
    arg_keys = jax.random.split(jax.random.key(seed), 7)
    tokens = bell_draw(arg_keys[0], (TOKENS, D), 1.0, 6.0, ((0, 32),))
    out_grad = bell_draw(arg_keys[1], (TOKENS, FF), 1.0, 6.0, ((0, 32),))
    weight_blocks = bell_draw(arg_keys[2], (NNZ, BS, BS), (NNZ * BS // (D // BS)) ** -0.5, 0.375, ((0, 8),))
    block_row = draw_block_row(jax.random.fold_in(arg_keys[6], 71), 0)
    block_col = draw_block_col(jax.random.fold_in(arg_keys[6], 71), 0)
    send_list = draw_send_list(jax.random.fold_in(arg_keys[6], 71), 0)
    return {"tokens": tokens, "out_grad": out_grad, "weight_blocks": weight_blocks, "block_row": block_row, "block_col": block_col, "send_list": send_list}


def reference(tokens, out_grad, weight_blocks, block_row, block_col, send_list):
    def input_step(running, block_index):
        row_start = block_row[block_index] * BS
        col_start = block_col[block_index] * BS
        columns = lax.dynamic_slice_in_dim(out_grad, col_start, BS, 1).astype(jnp.float32)
        weight = weight_blocks[block_index].astype(jnp.float32)
        update = jnp.dot(columns, weight.T, precision=lax.Precision.HIGHEST)
        current = lax.dynamic_slice_in_dim(running, row_start, BS, 1)
        return lax.dynamic_update_slice_in_dim(running, current + update, row_start, 1), None

    zero_grad = jnp.zeros((TOKENS, D), jnp.float32)
    summed, unused = lax.scan(input_step, zero_grad, jnp.arange(NNZ, dtype=jnp.int32))
    token_grad = summed.astype(jnp.bfloat16)

    def weight_step(block_index):
        row_start = block_row[block_index] * BS
        col_start = block_col[block_index] * BS
        left_cols = lax.dynamic_slice_in_dim(tokens, row_start, BS, 1).astype(jnp.float32)
        right_cols = lax.dynamic_slice_in_dim(out_grad, col_start, BS, 1).astype(jnp.float32)
        return jnp.dot(left_cols.T, right_cols, precision=lax.Precision.HIGHEST)

    block_grad = lax.map(weight_step, jnp.arange(NNZ, dtype=jnp.int32)) * (TOKENS ** -0.5)
    padded = jnp.concatenate([block_grad, jnp.zeros((1, BS, BS), jnp.float32)], axis=0)
    shard_base = (jnp.arange(N_FSDP, dtype=jnp.int32) * BLK_DEV)[:, None, None]
    global_index = jnp.where(send_list < BLK_DEV, shard_base + send_list, NNZ).astype(jnp.int32)
    owned_blocks = jnp.take(padded, global_index, axis=0)
    return token_grad, jnp.transpose(owned_blocks, (1, 0, 2, 3, 4))
```

```python
import functools

import jax
import jax.numpy as jnp
from jax import lax
from jax.experimental import pallas as pl
from jax.experimental.pallas import tpu as pltpu
from jax.sharding import PartitionSpec as P

MESH = pl.DeviceIdType.MESH


def exchange(
    reps, chips, cap, scale,
    rows_ref, cols_ref, list_ref, tokens_ref, grad_ref, weight_ref,
    gathered_ref, owned_ref,
    tok, grad, pair_out, pair_in, mine, chip_in, padded, rep_out, rep_in,
    load_sem, w_send, w_recv, fw_send, fw_recv, p_send, p_recv, c_send, c_recv, r_send, r_recv,
):
    rep = lax.axis_index("rep")
    shard = lax.axis_index("fsdp")
    chip, core = shard // 2, shard % 2
    other = chip * 2 + 1 - core
    per, size = weight_ref.shape[0], weight_ref.shape[1]

    def load(source, target, sem):
        def step(b, carry):
            place = pl.ds(pl.multiple_of(b * size, size), size)
            pltpu.make_async_copy(source.at[:, place], target.at[b], sem).start()
            return carry

        lax.fori_loop(0, target.shape[0], step, 0, unroll=8)

    load(tokens_ref, tok, load_sem.at[0])
    load(grad_ref, grad, load_sem.at[1])
    own_slot = gathered_ref.at[pl.ds(shard * per, per)]
    keep = pltpu.make_async_copy(weight_ref, own_slot, load_sem.at[2])
    keep.start()

    def at(d):
        return lax.rem(chip + d, chips)

    def back(d):
        return lax.rem(chip + chips - d, chips)

    barrier = pltpu.get_barrier_semaphore()
    pl.semaphore_signal(barrier, inc=1, device_id=(rep, other), device_id_type=MESH)
    for d in range(1, chips):
        pl.semaphore_signal(
            barrier, inc=1, device_id=(rep, at(d) * 2 + core), device_id_type=MESH
        )
    for d in range(1, reps):
        pl.semaphore_signal(
            barrier, inc=1, device_id=(lax.rem(rep + d, reps), shard), device_id_type=MESH
        )
    pl.semaphore_wait(barrier, chips + reps - 1)

    sends = []

    def remote(src, dst, send, recv, device):
        copy = pltpu.make_async_remote_copy(
            src_ref=src, dst_ref=dst, send_sem=send, recv_sem=recv,
            device_id=device, device_id_type=MESH,
        )
        copy.start()
        sends.append(copy)
        return copy

    forwards = [remote(weight_ref, own_slot, fw_send.at[0], fw_recv.at[0], (rep, other))]
    arrivals = [None]
    for d in range(1, chips):
        arrivals.append(
            remote(weight_ref, own_slot, w_send.at[d], w_recv.at[d], (rep, at(d) * 2 + core))
        )

    pltpu.make_async_copy(tok, tok, load_sem.at[0]).wait()
    pltpu.make_async_copy(grad, grad, load_sem.at[1]).wait()

    def products(first, target):
        def step(j, carry):
            target[j] = lax.dot_general(
                tok[rows_ref[first + j]], grad[cols_ref[first + j]],
                (((0,), (0,)), ((), ())), preferred_element_type=jnp.float32,
            )
            return carry

        lax.fori_loop(0, per, step, 0, unroll=True)

    order = list(range(1, chips)) + [0]
    pairs, chip_copies = {}, {}

    def finish(d):
        pairs[d].wait_recv()
        mine[d] = mine[d] + pair_in[d]
        if d:
            chip_copies[d] = remote(
                mine.at[d], chip_in.at[d], c_send.at[d], c_recv.at[d],
                (rep, at(d) * 2 + core),
            )

    for n, d in enumerate(order):
        products((at(d) * 2 + 1 - core) * per, pair_out.at[d])
        pairs[d] = remote(
            pair_out.at[d], pair_in.at[d], p_send.at[d], p_recv.at[d], (rep, other)
        )
        products((at(d) * 2 + core) * per, mine.at[d])
        if n:
            finish(order[n - 1])
    finish(0)

    for d in range(1, chips):
        arrivals[d].wait_recv()
        slot = gathered_ref.at[pl.ds((back(d) * 2 + core) * per, per)]
        forwards.append(
            remote(slot, slot, fw_send.at[d], fw_recv.at[d], (rep, other))
        )

    total = mine[0]
    for d in range(1, chips):
        chip_copies[d].wait_recv()
        total = total + chip_in[d]
    padded[:per] = total * scale
    padded[per] = jnp.zeros((size, size), jnp.float32)

    rep_copies = {}
    for d in range(1, reps):
        peer = lax.rem(rep + d, reps)
        for s in range(cap):
            rep_out[d, s] = padded[list_ref[peer * cap + s]]
        rep_copies[d] = remote(
            rep_out.at[d], rep_in.at[d], r_send.at[d], r_recv.at[d], (peer, shard)
        )
    for s in range(cap):
        owned_ref[s] = padded[list_ref[rep * cap + s]]
    for d in range(1, reps):
        rep_copies[d].wait_recv()
        owned_ref[...] = owned_ref[...] + rep_in[d]
    for copy in forwards:
        copy.wait_recv()
    for copy in sends:
        copy.wait_send()
    keep.wait()


def token_kernel(count, rows_ref, cols_ref, grad_ref, weight_ref, out_ref, total):
    size = weight_ref.shape[1]
    total[...] = jnp.zeros_like(total)

    def step(k, carry):
        col = pl.multiple_of(cols_ref[k] * size, size)
        row = rows_ref[k]
        total[row] = total[row] + lax.dot_general(
            grad_ref[:, pl.ds(col, size)], weight_ref[k],
            (((1,), (1,)), ((), ())), preferred_element_type=jnp.float32,
        )
        return carry

    lax.fori_loop(0, count, step, 0, unroll=8)
    for r in range(total.shape[0]):
        out_ref[:, r * size : (r + 1) * size] = total[r].astype(out_ref.dtype)


def local(tokens, out_grad, weight_blocks, block_row, block_col, send_list):
    rows_here, width = tokens.shape
    wide = out_grad.shape[1]
    per, size = weight_blocks.shape[:2]
    reps, shards = lax.axis_size("rep"), lax.axis_size("fsdp")
    chips, cap = shards // 2, send_list.shape[2]
    count = shards * per
    scale = float(rows_here * reps * shards) ** (-0.5)
    smem = pl.BlockSpec(memory_space=pltpu.SMEM)
    vmem = pl.BlockSpec(memory_space=pltpu.VMEM)
    hbm = pl.BlockSpec(memory_space=pl.ANY)
    f32 = jnp.float32
    dma = pltpu.SemaphoreType.DMA
    gathered, owned = pl.pallas_call(
        functools.partial(exchange, reps, chips, cap, scale),
        out_shape=(
            jax.ShapeDtypeStruct((count, size, size), weight_blocks.dtype),
            jax.ShapeDtypeStruct((cap, size, size), f32),
        ),
        in_specs=[smem, smem, smem, hbm, hbm, hbm],
        out_specs=(hbm, vmem),
        scratch_shapes=[
            pltpu.VMEM((width // size, rows_here, size), tokens.dtype),
            pltpu.VMEM((wide // size, rows_here, size), out_grad.dtype),
            pltpu.VMEM((chips, per, size, size), f32),
            pltpu.VMEM((chips, per, size, size), f32),
            pltpu.VMEM((chips, per, size, size), f32),
            pltpu.VMEM((chips, per, size, size), f32),
            pltpu.VMEM((per + 1, size, size), f32),
            pltpu.VMEM((reps, cap, size, size), f32),
            pltpu.VMEM((reps, cap, size, size), f32),
            dma((3,)), dma((chips,)), dma((chips,)), dma((chips,)), dma((chips,)),
            dma((chips,)), dma((chips,)), dma((chips,)), dma((chips,)),
            dma((reps,)), dma((reps,)),
        ],
        compiler_params=pltpu.CompilerParams(
            collective_id=0, has_side_effects=True, vmem_limit_bytes=56 * 2**20
        ),
    )(block_row, block_col, send_list.reshape(-1), tokens, out_grad, weight_blocks)
    token_grad = pl.pallas_call(
        functools.partial(token_kernel, count),
        out_shape=jax.ShapeDtypeStruct((rows_here, width), jnp.bfloat16),
        in_specs=[smem, smem, vmem, vmem],
        out_specs=vmem,
        scratch_shapes=[pltpu.VMEM((width // size, rows_here, size), f32)],
        compiler_params=pltpu.CompilerParams(vmem_limit_bytes=48 * 2**20),
    )(block_row, block_col, out_grad, gathered)
    return (token_grad, owned[None, None])


def solution(mesh):
    return jax.shard_map(
        local,
        mesh=mesh,
        in_specs=(
            P(("rep", "fsdp"), None),
            P(("rep", "fsdp"), None),
            P("fsdp", None, None),
            P(),
            P(),
            P("fsdp", None, None),
        ),
        out_specs=(P(("rep", "fsdp"), None), P("rep", "fsdp", None, None, None)),
        check_vma=False,
    )
```

```python
import functools

import jax
import jax.numpy as jnp
from jax import lax
from jax.experimental import pallas as pl
from jax.experimental.pallas import tpu as pltpu
from jax.sharding import PartitionSpec as P

MESH = pl.DeviceIdType.MESH


def exchange(
    reps, chips, cap, scale, fused,
    rows_ref, cols_ref, list_ref, chain_ref, tokens_ref, grad_ref, weight_ref,
    result_ref, owned_ref,
    tok, grad, pair_out, pair_in, mine, chip_in, padded, rep_out, rep_in,
    load_sem, w_send, w_recv, fw_send, fw_recv, p_send, p_recv, c_send, c_recv, r_send, r_recv,
    *inside,
):
    gathered_ref = inside[0] if fused else result_ref
    rep = lax.axis_index("rep")
    shard = lax.axis_index("fsdp")
    chip, core = shard // 2, shard % 2
    other = chip * 2 + 1 - core
    per, size = weight_ref.shape[0], weight_ref.shape[1]

    def load(source, target, sem):
        def step(b, carry):
            place = pl.ds(pl.multiple_of(b * size, size), size)
            pltpu.make_async_copy(source.at[:, place], target.at[b], sem).start()
            return carry

        lax.fori_loop(0, target.shape[0], step, 0, unroll=8)

    load(tokens_ref, tok, load_sem.at[0])
    load(grad_ref, grad, load_sem.at[1])
    own_slot = gathered_ref.at[pl.ds(shard * per, per)]
    keep = pltpu.make_async_copy(weight_ref, own_slot, load_sem.at[2])
    keep.start()

    def at(d):
        return lax.rem(chip + d, chips)

    def back(d):
        return lax.rem(chip + chips - d, chips)

    barrier = pltpu.get_barrier_semaphore()
    pl.semaphore_signal(barrier, inc=1, device_id=(rep, other), device_id_type=MESH)
    for d in range(1, chips):
        pl.semaphore_signal(
            barrier, inc=1, device_id=(rep, at(d) * 2 + core), device_id_type=MESH
        )
    for d in range(1, reps):
        pl.semaphore_signal(
            barrier, inc=1, device_id=(lax.rem(rep + d, reps), shard), device_id_type=MESH
        )
    pl.semaphore_wait(barrier, chips + reps - 1)

    sends = []

    def remote(src, dst, send, recv, device):
        copy = pltpu.make_async_remote_copy(
            src_ref=src, dst_ref=dst, send_sem=send, recv_sem=recv,
            device_id=device, device_id_type=MESH,
        )
        copy.start()
        sends.append(copy)
        return copy

    forwards = [remote(weight_ref, own_slot, fw_send.at[0], fw_recv.at[0], (rep, other))]
    arrivals = [None]
    for d in range(1, chips):
        arrivals.append(
            remote(weight_ref, own_slot, w_send.at[d], w_recv.at[d], (rep, at(d) * 2 + core))
        )

    pltpu.make_async_copy(tok, tok, load_sem.at[0]).wait()
    pltpu.make_async_copy(grad, grad, load_sem.at[1]).wait()

    def products(first, target):
        def step(j, carry):
            target[j] = lax.dot_general(
                tok[rows_ref[first + j]], grad[cols_ref[first + j]],
                (((0,), (0,)), ((), ())), preferred_element_type=jnp.float32,
            )
            return carry

        lax.fori_loop(0, per, step, 0, unroll=True)

    order = list(range(1, chips)) + [0]
    pairs, chip_copies = {}, {}

    def finish(d):
        pairs[d].wait_recv()
        mine[d] = mine[d] + pair_in[d]
        if d:
            chip_copies[d] = remote(
                mine.at[d], chip_in.at[d], c_send.at[d], c_recv.at[d],
                (rep, at(d) * 2 + core),
            )

    for n, d in enumerate(order):
        products((at(d) * 2 + 1 - core) * per, pair_out.at[d])
        pairs[d] = remote(
            pair_out.at[d], pair_in.at[d], p_send.at[d], p_recv.at[d], (rep, other)
        )
        products((at(d) * 2 + core) * per, mine.at[d])
        if n:
            finish(order[n - 1])
    finish(0)

    for d in range(1, chips):
        arrivals[d].wait_recv()
        slot = gathered_ref.at[pl.ds((back(d) * 2 + core) * per, per)]
        forwards.append(
            remote(slot, slot, fw_send.at[d], fw_recv.at[d], (rep, other))
        )

    if fused:
        _, running, out = inside
        count = running.shape[0] - 1
        running[count] = jnp.zeros(running.shape[1:], jnp.float32)
        for copy in forwards:
            copy.wait_recv()
        keep.wait()

        def chained(k, carry):
            running[k] = running[chain_ref[k]] + lax.dot_general(
                grad[cols_ref[k]], gathered_ref[k],
                (((1,), (1,)), ((), ())), preferred_element_type=jnp.float32,
            )
            return carry

        lax.fori_loop(0, count, chained, 0, unroll=8)
        for r in range(out.shape[1] // size):
            out[:, r * size : (r + 1) * size] = running[chain_ref[count + r]].astype(out.dtype)
        store = pltpu.make_async_copy(out, result_ref, load_sem.at[3])
        store.start()

    total = mine[0]
    for d in range(1, chips):
        chip_copies[d].wait_recv()
        total = total + chip_in[d]
    padded[:per] = total * scale
    padded[per] = jnp.zeros((size, size), jnp.float32)

    rep_copies = {}
    for d in range(1, reps):
        peer = lax.rem(rep + d, reps)
        for s in range(cap):
            rep_out[d, s] = padded[list_ref[0, peer, s]]
        rep_copies[d] = remote(
            rep_out.at[d], rep_in.at[d], r_send.at[d], r_recv.at[d], (peer, shard)
        )
    for s in range(cap):
        owned_ref[s] = padded[list_ref[0, rep, s]]
    for d in range(1, reps):
        rep_copies[d].wait_recv()
        owned_ref[...] = owned_ref[...] + rep_in[d]
    for copy in sends:
        copy.wait_send()
    if fused:
        store.wait()
    else:
        for copy in forwards:
            copy.wait_recv()
        keep.wait()


def token_kernel(count, rows_ref, cols_ref, grad_ref, weight_ref, out_ref, total):
    size = weight_ref.shape[1]
    total[...] = jnp.zeros_like(total)

    def step(k, carry):
        col = pl.multiple_of(cols_ref[k] * size, size)
        row = rows_ref[k]
        total[row] = total[row] + lax.dot_general(
            grad_ref[:, pl.ds(col, size)], weight_ref[k],
            (((1,), (1,)), ((), ())), preferred_element_type=jnp.float32,
        )
        return carry

    lax.fori_loop(0, count, step, 0, unroll=8)
    for r in range(total.shape[0]):
        out_ref[:, r * size : (r + 1) * size] = total[r].astype(out_ref.dtype)


def local(tokens, out_grad, weight_blocks, block_row, block_col, send_list):
    rows_here, width = tokens.shape
    wide = out_grad.shape[1]
    per, size = weight_blocks.shape[:2]
    reps, shards = lax.axis_size("rep"), lax.axis_size("fsdp")
    chips, cap = shards // 2, send_list.shape[2]
    count = shards * per
    scale = float(rows_here * reps * shards) ** (-0.5)
    smem = pl.BlockSpec(memory_space=pltpu.SMEM)
    vmem = pl.BlockSpec(memory_space=pltpu.VMEM)
    hbm = pl.BlockSpec(memory_space=pl.ANY)
    f32 = jnp.float32
    dma = pltpu.SemaphoreType.DMA
    gathered_shape = (count, size, size)
    inside, fused = [], count * rows_here * size * 4 <= 12 * 2**20
    chain = block_row
    result_shape = jax.ShapeDtypeStruct(gathered_shape, weight_blocks.dtype)
    if fused:
        row_total = width // size
        result_shape = jax.ShapeDtypeStruct((rows_here, width), jnp.bfloat16)
        inside = [
            pltpu.VMEM(gathered_shape, weight_blocks.dtype),
            pltpu.VMEM((count + 1, rows_here, size), f32),
            pltpu.VMEM((rows_here, width), jnp.bfloat16),
        ]
        serial = jnp.arange(count, dtype=jnp.int32)
        keys = jnp.concatenate([block_row, jnp.arange(row_total, dtype=jnp.int32)])
        ends = jnp.minimum(jnp.arange(count + row_total, dtype=jnp.int32), count)
        found = (keys[:, None] == block_row[None, :]) & (serial[None, :] < ends[:, None])
        latest = jnp.max(jnp.where(found, serial[None, :], -1), axis=1)
        chain = jnp.where(latest < 0, count, latest)
    result, owned = pl.pallas_call(
        functools.partial(exchange, reps, chips, cap, scale, fused),
        out_shape=(
            result_shape,
            jax.ShapeDtypeStruct((cap, size, size), f32),
        ),
        in_specs=[smem, smem, smem, smem, hbm, hbm, hbm],
        out_specs=(hbm, vmem),
        scratch_shapes=[
            pltpu.VMEM((width // size, rows_here, size), tokens.dtype),
            pltpu.VMEM((wide // size, rows_here, size), out_grad.dtype),
            pltpu.VMEM((chips, per, size, size), f32),
            pltpu.VMEM((chips, per, size, size), f32),
            pltpu.VMEM((chips, per, size, size), f32),
            pltpu.VMEM((chips, per, size, size), f32),
            pltpu.VMEM((per + 1, size, size), f32),
            pltpu.VMEM((reps, cap, size, size), f32),
            pltpu.VMEM((reps, cap, size, size), f32),
            dma((4,)), dma((chips,)), dma((chips,)), dma((chips,)), dma((chips,)),
            dma((chips,)), dma((chips,)), dma((chips,)), dma((chips,)),
            dma((reps,)), dma((reps,)),
            *inside,
        ],
        compiler_params=pltpu.CompilerParams(
            collective_id=0, has_side_effects=True, vmem_limit_bytes=56 * 2**20
        ),
    )(block_row, block_col, send_list, chain, tokens, out_grad, weight_blocks)
    if fused:
        return (result, owned[None, None])
    token_grad = pl.pallas_call(
        functools.partial(token_kernel, count),
        out_shape=jax.ShapeDtypeStruct((rows_here, width), jnp.bfloat16),
        in_specs=[smem, smem, vmem, vmem],
        out_specs=vmem,
        scratch_shapes=[pltpu.VMEM((width // size, rows_here, size), f32)],
        compiler_params=pltpu.CompilerParams(vmem_limit_bytes=48 * 2**20),
    )(block_row, block_col, out_grad, result)
    return (token_grad, owned[None, None])


def solution(mesh):
    return jax.shard_map(
        local,
        mesh=mesh,
        in_specs=(
            P(("rep", "fsdp"), None),
            P(("rep", "fsdp"), None),
            P("fsdp", None, None),
            P(),
            P(),
            P("fsdp", None, None),
        ),
        out_specs=(P(("rep", "fsdp"), None), P("rep", "fsdp", None, None, None)),
        check_vma=False,
    )
```

```python
import functools

import jax
import jax.numpy as jnp
from jax import lax
from jax.experimental import pallas as pl
from jax.experimental.pallas import tpu as pltpu
from jax.sharding import PartitionSpec as P

MESH = pl.DeviceIdType.MESH


LEVELS = 32767.0


def encode(values):
    top = jnp.maximum(jnp.max(jnp.abs(values), axis=1), 1e-30)
    codes = jnp.round(values * (LEVELS / top)[:, None, :])
    return codes.astype(jnp.int32).astype(jnp.int16), top * (1.0 / LEVELS)


def decode(codes, unit):
    return codes.astype(jnp.int32).astype(jnp.float32) * unit[:, None, :]


def exchange(
    reps, chips, cap, scale, fused,
    rows_ref, cols_ref, list_ref, chain_ref, tokens_ref, grad_ref, weight_ref,
    result_ref, owned_ref,
    tok, grad, pair_out, pair_in, mine, chip_out, chip_in, chip_unit_out, chip_unit_in,
    padded, codes, units, rep_out, rep_in, rep_unit_out, rep_unit_in,
    load_sem, w_send, w_recv, fw_send, fw_recv, p_send, p_recv, c_send, c_recv, r_send, r_recv,
    cu_send, cu_recv, ru_send, ru_recv,
    *inside,
):
    gathered_ref = inside[0] if fused else result_ref
    rep = lax.axis_index("rep")
    shard = lax.axis_index("fsdp")
    chip, core = shard // 2, shard % 2
    other = chip * 2 + 1 - core
    per, size = weight_ref.shape[0], weight_ref.shape[1]

    def load(source, target, sem):
        def step(b, carry):
            place = pl.ds(pl.multiple_of(b * size, size), size)
            pltpu.make_async_copy(source.at[:, place], target.at[b], sem).start()
            return carry

        lax.fori_loop(0, target.shape[0], step, 0, unroll=8)

    load(tokens_ref, tok, load_sem.at[0])
    load(grad_ref, grad, load_sem.at[1])
    own_slot = gathered_ref.at[pl.ds(shard * per, per)]
    keep = pltpu.make_async_copy(weight_ref, own_slot, load_sem.at[2])
    keep.start()

    def at(d):
        return lax.rem(chip + d, chips)

    def back(d):
        return lax.rem(chip + chips - d, chips)

    barrier = pltpu.get_barrier_semaphore()
    pl.semaphore_signal(barrier, inc=1, device_id=(rep, other), device_id_type=MESH)
    for d in range(1, chips):
        pl.semaphore_signal(
            barrier, inc=1, device_id=(rep, at(d) * 2 + core), device_id_type=MESH
        )
    for d in range(1, reps):
        pl.semaphore_signal(
            barrier, inc=1, device_id=(lax.rem(rep + d, reps), shard), device_id_type=MESH
        )
    pl.semaphore_wait(barrier, chips + reps - 1)

    sends = []

    def remote(src, dst, send, recv, device):
        copy = pltpu.make_async_remote_copy(
            src_ref=src, dst_ref=dst, send_sem=send, recv_sem=recv,
            device_id=device, device_id_type=MESH,
        )
        copy.start()
        sends.append(copy)
        return copy

    forwards = [remote(weight_ref, own_slot, fw_send.at[0], fw_recv.at[0], (rep, other))]
    arrivals = [None]
    for d in range(1, chips):
        arrivals.append(
            remote(weight_ref, own_slot, w_send.at[d], w_recv.at[d], (rep, at(d) * 2 + core))
        )

    pltpu.make_async_copy(tok, tok, load_sem.at[0]).wait()
    pltpu.make_async_copy(grad, grad, load_sem.at[1]).wait()

    def products(first, target):
        def step(j, carry):
            target[j] = lax.dot_general(
                tok[rows_ref[first + j]], grad[cols_ref[first + j]],
                (((0,), (0,)), ((), ())), preferred_element_type=jnp.float32,
            )
            return carry

        lax.fori_loop(0, per, step, 0, unroll=True)

    order = list(range(1, chips)) + [0]
    pairs, chip_copies = {}, {}

    def finish(d):
        pairs[d].wait_recv()
        mine[d] = mine[d] + pair_in[d]
        if d:
            device = (rep, at(d) * 2 + core)
            chip_out[d], chip_unit_out[d] = encode(mine[d])
            chip_copies[d] = (
                remote(chip_unit_out.at[d], chip_unit_in.at[d], cu_send.at[d], cu_recv.at[d], device),
                remote(chip_out.at[d], chip_in.at[d], c_send.at[d], c_recv.at[d], device),
            )

    for n, d in enumerate(order):
        products((at(d) * 2 + 1 - core) * per, pair_out.at[d])
        pairs[d] = remote(
            pair_out.at[d], pair_in.at[d], p_send.at[d], p_recv.at[d], (rep, other)
        )
        products((at(d) * 2 + core) * per, mine.at[d])
        if n:
            finish(order[n - 1])
    finish(0)

    for d in range(1, chips):
        arrivals[d].wait_recv()
        slot = gathered_ref.at[pl.ds((back(d) * 2 + core) * per, per)]
        forwards.append(
            remote(slot, slot, fw_send.at[d], fw_recv.at[d], (rep, other))
        )

    if fused:
        _, running, out = inside
        count = running.shape[0] - 1
        running[count] = jnp.zeros(running.shape[1:], jnp.float32)
        for copy in forwards:
            copy.wait_recv()
        keep.wait()

        def chained(k, carry):
            running[k] = running[chain_ref[k]] + lax.dot_general(
                grad[cols_ref[k]], gathered_ref[k],
                (((1,), (1,)), ((), ())), preferred_element_type=jnp.float32,
            )
            return carry

        lax.fori_loop(0, count, chained, 0, unroll=8)
        for r in range(out.shape[1] // size):
            out[:, r * size : (r + 1) * size] = running[chain_ref[count + r]].astype(out.dtype)
        store = pltpu.make_async_copy(out, result_ref, load_sem.at[3])
        store.start()

    total = mine[0]
    for d in range(1, chips):
        for copy in chip_copies[d]:
            copy.wait_recv()
        total = total + decode(chip_in[d], chip_unit_in[d])
    total = total * scale
    padded[:per] = total
    padded[per] = jnp.zeros((size, size), jnp.float32)
    codes[:per], units[:per] = encode(total)
    codes[per] = jnp.zeros((size, size), jnp.int16)
    units[per:] = jnp.zeros((units.shape[0] - per, size), jnp.float32)

    rep_copies = {}
    for d in range(1, reps):
        peer = lax.rem(rep + d, reps)
        for s in range(cap):
            rep_out[d, s] = codes[list_ref[0, peer, s]]
            rep_unit_out[d, s] = units[list_ref[0, peer, s]]
        device = (peer, shard)
        rep_copies[d] = (
            remote(rep_unit_out.at[d], rep_unit_in.at[d], ru_send.at[d], ru_recv.at[d], device),
            remote(rep_out.at[d], rep_in.at[d], r_send.at[d], r_recv.at[d], device),
        )
    for s in range(cap):
        owned_ref[s] = padded[list_ref[0, rep, s]]
    for d in range(1, reps):
        for copy in rep_copies[d]:
            copy.wait_recv()
        owned_ref[...] = owned_ref[...] + decode(rep_in[d], rep_unit_in[d])
    for copy in sends:
        copy.wait_send()
    if fused:
        store.wait()
    else:
        for copy in forwards:
            copy.wait_recv()
        keep.wait()


def token_kernel(count, rows_ref, cols_ref, grad_ref, weight_ref, out_ref, total):
    size = weight_ref.shape[1]
    total[...] = jnp.zeros_like(total)

    def step(k, carry):
        col = pl.multiple_of(cols_ref[k] * size, size)
        row = rows_ref[k]
        total[row] = total[row] + lax.dot_general(
            grad_ref[:, pl.ds(col, size)], weight_ref[k],
            (((1,), (1,)), ((), ())), preferred_element_type=jnp.float32,
        )
        return carry

    lax.fori_loop(0, count, step, 0, unroll=8)
    for r in range(total.shape[0]):
        out_ref[:, r * size : (r + 1) * size] = total[r].astype(out_ref.dtype)


def local(tokens, out_grad, weight_blocks, block_row, block_col, send_list):
    rows_here, width = tokens.shape
    wide = out_grad.shape[1]
    per, size = weight_blocks.shape[:2]
    reps, shards = lax.axis_size("rep"), lax.axis_size("fsdp")
    chips, cap = shards // 2, send_list.shape[2]
    count = shards * per
    scale = float(rows_here * reps * shards) ** (-0.5)
    smem = pl.BlockSpec(memory_space=pltpu.SMEM)
    vmem = pl.BlockSpec(memory_space=pltpu.VMEM)
    hbm = pl.BlockSpec(memory_space=pl.ANY)
    f32 = jnp.float32
    dma = pltpu.SemaphoreType.DMA
    gathered_shape = (count, size, size)
    inside, fused = [], count * rows_here * size * 4 <= 12 * 2**20
    chain = block_row
    result_shape = jax.ShapeDtypeStruct(gathered_shape, weight_blocks.dtype)
    if fused:
        row_total = width // size
        result_shape = jax.ShapeDtypeStruct((rows_here, width), jnp.bfloat16)
        inside = [
            pltpu.VMEM(gathered_shape, weight_blocks.dtype),
            pltpu.VMEM((count + 1, rows_here, size), f32),
            pltpu.VMEM((rows_here, width), jnp.bfloat16),
        ]
        serial = jnp.arange(count, dtype=jnp.int32)
        keys = jnp.concatenate([block_row, jnp.arange(row_total, dtype=jnp.int32)])
        ends = jnp.minimum(jnp.arange(count + row_total, dtype=jnp.int32), count)
        found = (keys[:, None] == block_row[None, :]) & (serial[None, :] < ends[:, None])
        latest = jnp.max(jnp.where(found, serial[None, :], -1), axis=1)
        chain = jnp.where(latest < 0, count, latest)
    result, owned = pl.pallas_call(
        functools.partial(exchange, reps, chips, cap, scale, fused),
        out_shape=(
            result_shape,
            jax.ShapeDtypeStruct((cap, size, size), f32),
        ),
        in_specs=[smem, smem, smem, smem, hbm, hbm, hbm],
        out_specs=(hbm, vmem),
        scratch_shapes=[
            pltpu.VMEM((width // size, rows_here, size), tokens.dtype),
            pltpu.VMEM((wide // size, rows_here, size), out_grad.dtype),
            pltpu.VMEM((chips, per, size, size), f32),
            pltpu.VMEM((chips, per, size, size), f32),
            pltpu.VMEM((chips, per, size, size), f32),
            pltpu.VMEM((chips, per, size, size), jnp.int16),
            pltpu.VMEM((chips, per, size, size), jnp.int16),
            pltpu.VMEM((chips, per, size), f32),
            pltpu.VMEM((chips, per, size), f32),
            pltpu.VMEM((per + 1, size, size), f32),
            pltpu.VMEM((per + 1, size, size), jnp.int16),
            pltpu.VMEM((per + 8, size), f32),
            pltpu.VMEM((reps, cap, size, size), jnp.int16),
            pltpu.VMEM((reps, cap, size, size), jnp.int16),
            pltpu.VMEM((reps, cap, size), f32),
            pltpu.VMEM((reps, cap, size), f32),
            dma((4,)), dma((chips,)), dma((chips,)), dma((chips,)), dma((chips,)),
            dma((chips,)), dma((chips,)), dma((chips,)), dma((chips,)),
            dma((reps,)), dma((reps,)),
            dma((chips,)), dma((chips,)), dma((reps,)), dma((reps,)),
            *inside,
        ],
        compiler_params=pltpu.CompilerParams(
            collective_id=0, has_side_effects=True, vmem_limit_bytes=56 * 2**20
        ),
    )(block_row, block_col, send_list, chain, tokens, out_grad, weight_blocks)
    if fused:
        return (result, owned[None, None])
    token_grad = pl.pallas_call(
        functools.partial(token_kernel, count),
        out_shape=jax.ShapeDtypeStruct((rows_here, width), jnp.bfloat16),
        in_specs=[smem, smem, vmem, vmem],
        out_specs=vmem,
        scratch_shapes=[pltpu.VMEM((width // size, rows_here, size), f32)],
        compiler_params=pltpu.CompilerParams(vmem_limit_bytes=48 * 2**20),
    )(block_row, block_col, out_grad, result)
    return (token_grad, owned[None, None])


def solution(mesh):
    return jax.shard_map(
        local,
        mesh=mesh,
        in_specs=(
            P(("rep", "fsdp"), None),
            P(("rep", "fsdp"), None),
            P("fsdp", None, None),
            P(),
            P(),
            P("fsdp", None, None),
        ),
        out_specs=(P(("rep", "fsdp"), None), P("rep", "fsdp", None, None, None)),
        check_vma=False,
    )
```

```python
import functools

import jax
import jax.numpy as jnp
from jax import lax
from jax.experimental import pallas as pl
from jax.experimental.pallas import tpu as pltpu
from jax.sharding import PartitionSpec as P

MESH = pl.DeviceIdType.MESH


LEVELS = 32767.0


def encode(values):
    top = jnp.maximum(jnp.max(jnp.abs(values), axis=1), 1e-30)
    codes = jnp.round(values * (LEVELS / top)[:, None, :])
    return codes.astype(jnp.int32).astype(jnp.int16), top * (1.0 / LEVELS)


def decode(codes, unit):
    return codes.astype(jnp.int32).astype(jnp.float32) * unit[:, None, :]


def exchange(
    reps, chips, cap, scale, fused,
    rows_ref, cols_ref, list_ref, chain_ref, tokens_ref, grad_ref, weight_ref,
    result_ref, owned_ref,
    tok, grad, pair_out, pair_in, mine, chip_out, chip_in, chip_unit_out, chip_unit_in,
    padded, codes, units, rep_out, rep_in, rep_unit_out, rep_unit_in,
    load_sem, w_send, w_recv, fw_send, fw_recv, p_send, p_recv, c_send, c_recv, r_send, r_recv,
    cu_send, cu_recv, ru_send, ru_recv,
    *inside,
):
    gathered_ref = inside[0] if fused else result_ref
    rep = lax.axis_index("rep")
    shard = lax.axis_index("fsdp")
    chip, core = shard // 2, shard % 2
    other = chip * 2 + 1 - core
    per, size = weight_ref.shape[0], weight_ref.shape[1]

    def load(source, target, sem):
        def step(b, carry):
            place = pl.ds(pl.multiple_of(b * size, size), size)
            pltpu.make_async_copy(source.at[:, place], target.at[b], sem).start()
            return carry

        lax.fori_loop(0, target.shape[0], step, 0, unroll=8)

    load(tokens_ref, tok, load_sem.at[0])
    load(grad_ref, grad, load_sem.at[1])
    own_slot = gathered_ref.at[pl.ds(shard * per, per)]
    keep = pltpu.make_async_copy(weight_ref, own_slot, load_sem.at[2])
    keep.start()

    def at(d):
        return lax.rem(chip + d, chips)

    def back(d):
        return lax.rem(chip + chips - d, chips)

    barrier = pltpu.get_barrier_semaphore()
    pl.semaphore_signal(barrier, inc=1, device_id=(rep, other), device_id_type=MESH)
    for d in range(1, chips):
        pl.semaphore_signal(
            barrier, inc=1, device_id=(rep, at(d) * 2 + core), device_id_type=MESH
        )
    for d in range(1, reps):
        pl.semaphore_signal(
            barrier, inc=1, device_id=(lax.rem(rep + d, reps), shard), device_id_type=MESH
        )
    pl.semaphore_wait(barrier, chips + reps - 1)

    sends = []

    def remote(src, dst, send, recv, device):
        copy = pltpu.make_async_remote_copy(
            src_ref=src, dst_ref=dst, send_sem=send, recv_sem=recv,
            device_id=device, device_id_type=MESH,
        )
        copy.start()
        sends.append(copy)
        return copy

    forwards = [remote(weight_ref, own_slot, fw_send.at[0], fw_recv.at[0], (rep, other))]
    arrivals = [None]
    for d in range(1, chips):
        arrivals.append(
            remote(weight_ref, own_slot, w_send.at[d], w_recv.at[d], (rep, at(d) * 2 + core))
        )

    pltpu.make_async_copy(tok, tok, load_sem.at[0]).wait()
    pltpu.make_async_copy(grad, grad, load_sem.at[1]).wait()

    def products(first, target):
        def step(j, carry):
            target[j] = lax.dot_general(
                tok[rows_ref[first + j]], grad[cols_ref[first + j]],
                (((0,), (0,)), ((), ())), preferred_element_type=jnp.float32,
            )
            return carry

        lax.fori_loop(0, per, step, 0, unroll=True)

    order = list(range(1, chips)) + [0]
    pairs, chip_copies = {}, {}

    def finish(d):
        pairs[d].wait_recv()
        mine[d] = mine[d] + pair_in[d]
        if d:
            device = (rep, at(d) * 2 + core)
            chip_out[d], chip_unit_out[d] = encode(mine[d])
            chip_copies[d] = (
                remote(chip_unit_out.at[d], chip_unit_in.at[d], cu_send.at[d], cu_recv.at[d], device),
                remote(chip_out.at[d], chip_in.at[d], c_send.at[d], c_recv.at[d], device),
            )

    for n, d in enumerate(order):
        products((at(d) * 2 + 1 - core) * per, pair_out.at[d])
        pairs[d] = remote(
            pair_out.at[d], pair_in.at[d], p_send.at[d], p_recv.at[d], (rep, other)
        )
        products((at(d) * 2 + core) * per, mine.at[d])
        if n:
            finish(order[n - 1])
    finish(0)

    for d in range(1, chips):
        arrivals[d].wait_recv()
        slot = gathered_ref.at[pl.ds((back(d) * 2 + core) * per, per)]
        forwards.append(
            remote(slot, slot, fw_send.at[d], fw_recv.at[d], (rep, other))
        )

    total = mine[0]
    for d in range(1, chips):
        for copy in chip_copies[d]:
            copy.wait_recv()
        total = total + decode(chip_in[d], chip_unit_in[d])
    total = total * scale
    padded[:per] = total
    padded[per] = jnp.zeros((size, size), jnp.float32)
    codes[:per], units[:per] = encode(total)
    codes[per] = jnp.zeros((size, size), jnp.int16)
    units[per:] = jnp.zeros((units.shape[0] - per, size), jnp.float32)

    rep_copies = {}
    for d in range(1, reps):
        peer = lax.rem(rep + d, reps)
        for s in range(cap):
            rep_out[d, s] = codes[list_ref[0, peer, s]]
            rep_unit_out[d, s] = units[list_ref[0, peer, s]]
        device = (peer, shard)
        rep_copies[d] = (
            remote(rep_unit_out.at[d], rep_unit_in.at[d], ru_send.at[d], ru_recv.at[d], device),
            remote(rep_out.at[d], rep_in.at[d], r_send.at[d], r_recv.at[d], device),
        )
    if fused:
        _, running = inside
        out = result_ref
        count = running.shape[0] - 1
        running[count] = jnp.zeros(running.shape[1:], jnp.float32)
        for copy in forwards:
            copy.wait_recv()
        keep.wait()

        def chained(k, carry):
            running[k] = running[chain_ref[k]] + lax.dot_general(
                grad[cols_ref[k]], gathered_ref[k],
                (((1,), (1,)), ((), ())), preferred_element_type=jnp.float32,
            )
            return carry

        lax.fori_loop(0, count, chained, 0, unroll=8)
        for r in range(out.shape[1] // size):
            out[:, r * size : (r + 1) * size] = running[chain_ref[count + r]].astype(out.dtype)

    for s in range(cap):
        owned_ref[s] = padded[list_ref[0, rep, s]]
    for d in range(1, reps):
        for copy in rep_copies[d]:
            copy.wait_recv()
        owned_ref[...] = owned_ref[...] + decode(rep_in[d], rep_unit_in[d])
    for copy in sends:
        copy.wait_send()
    if not fused:
        for copy in forwards:
            copy.wait_recv()
        keep.wait()


def token_kernel(count, rows_ref, cols_ref, grad_ref, weight_ref, out_ref, total):
    size = weight_ref.shape[1]
    total[...] = jnp.zeros_like(total)

    def step(k, carry):
        col = pl.multiple_of(cols_ref[k] * size, size)
        row = rows_ref[k]
        total[row] = total[row] + lax.dot_general(
            grad_ref[:, pl.ds(col, size)], weight_ref[k],
            (((1,), (1,)), ((), ())), preferred_element_type=jnp.float32,
        )
        return carry

    lax.fori_loop(0, count, step, 0, unroll=8)
    for r in range(total.shape[0]):
        out_ref[:, r * size : (r + 1) * size] = total[r].astype(out_ref.dtype)


def local(tokens, out_grad, weight_blocks, block_row, block_col, send_list):
    rows_here, width = tokens.shape
    wide = out_grad.shape[1]
    per, size = weight_blocks.shape[:2]
    reps, shards = lax.axis_size("rep"), lax.axis_size("fsdp")
    chips, cap = shards // 2, send_list.shape[2]
    count = shards * per
    scale = float(rows_here * reps * shards) ** (-0.5)
    smem = pl.BlockSpec(memory_space=pltpu.SMEM)
    vmem = pl.BlockSpec(memory_space=pltpu.VMEM)
    hbm = pl.BlockSpec(memory_space=pl.ANY)
    f32 = jnp.float32
    dma = pltpu.SemaphoreType.DMA
    gathered_shape = (count, size, size)
    inside, fused = [], count * rows_here * size * 4 <= 12 * 2**20
    chain = block_row
    result_shape = jax.ShapeDtypeStruct(gathered_shape, weight_blocks.dtype)
    if fused:
        row_total = width // size
        result_shape = pltpu.VMEM((rows_here, width), jnp.bfloat16)
        inside = [
            pltpu.VMEM(gathered_shape, weight_blocks.dtype),
            pltpu.VMEM((count + 1, rows_here, size), f32),
        ]
        serial = jnp.arange(count, dtype=jnp.int32)
        keys = jnp.concatenate([block_row, jnp.arange(row_total, dtype=jnp.int32)])
        ends = jnp.minimum(jnp.arange(count + row_total, dtype=jnp.int32), count)
        found = (keys[:, None] == block_row[None, :]) & (serial[None, :] < ends[:, None])
        latest = jnp.max(jnp.where(found, serial[None, :], -1), axis=1)
        chain = jnp.where(latest < 0, count, latest)
    result, owned = pl.pallas_call(
        functools.partial(exchange, reps, chips, cap, scale, fused),
        out_shape=(
            result_shape,
            jax.ShapeDtypeStruct((cap, size, size), f32),
        ),
        in_specs=[smem, smem, smem, smem, hbm, hbm, hbm],
        out_specs=(vmem if fused else hbm, vmem),
        scratch_shapes=[
            pltpu.VMEM((width // size, rows_here, size), tokens.dtype),
            pltpu.VMEM((wide // size, rows_here, size), out_grad.dtype),
            pltpu.VMEM((chips, per, size, size), f32),
            pltpu.VMEM((chips, per, size, size), f32),
            pltpu.VMEM((chips, per, size, size), f32),
            pltpu.VMEM((chips, per, size, size), jnp.int16),
            pltpu.VMEM((chips, per, size, size), jnp.int16),
            pltpu.VMEM((chips, per, size), f32),
            pltpu.VMEM((chips, per, size), f32),
            pltpu.VMEM((per + 1, size, size), f32),
            pltpu.VMEM((per + 1, size, size), jnp.int16),
            pltpu.VMEM((per + 8, size), f32),
            pltpu.VMEM((reps, cap, size, size), jnp.int16),
            pltpu.VMEM((reps, cap, size, size), jnp.int16),
            pltpu.VMEM((reps, cap, size), f32),
            pltpu.VMEM((reps, cap, size), f32),
            dma((3,)), dma((chips,)), dma((chips,)), dma((chips,)), dma((chips,)),
            dma((chips,)), dma((chips,)), dma((chips,)), dma((chips,)),
            dma((reps,)), dma((reps,)),
            dma((chips,)), dma((chips,)), dma((reps,)), dma((reps,)),
            *inside,
        ],
        compiler_params=pltpu.CompilerParams(
            collective_id=0, has_side_effects=True, vmem_limit_bytes=56 * 2**20
        ),
    )(block_row, block_col, send_list, chain, tokens, out_grad, weight_blocks)
    if fused:
        return (result, owned[None, None])
    token_grad = pl.pallas_call(
        functools.partial(token_kernel, count),
        out_shape=jax.ShapeDtypeStruct((rows_here, width), jnp.bfloat16),
        in_specs=[smem, smem, vmem, vmem],
        out_specs=vmem,
        scratch_shapes=[pltpu.VMEM((width // size, rows_here, size), f32)],
        compiler_params=pltpu.CompilerParams(vmem_limit_bytes=48 * 2**20),
    )(block_row, block_col, out_grad, result)
    return (token_grad, owned[None, None])


def solution(mesh):
    return jax.shard_map(
        local,
        mesh=mesh,
        in_specs=(
            P(("rep", "fsdp"), None),
            P(("rep", "fsdp"), None),
            P("fsdp", None, None),
            P(),
            P(),
            P("fsdp", None, None),
        ),
        out_specs=(P(("rep", "fsdp"), None), P("rep", "fsdp", None, None, None)),
        check_vma=False,
    )
```

```python
import functools

import jax
import jax.numpy as jnp
from jax import lax
from jax.experimental import pallas as pl
from jax.experimental.pallas import tpu as pltpu
from jax.sharding import PartitionSpec as P

MESH = pl.DeviceIdType.MESH


LEVELS = 32767.0


def encode(values):
    top = jnp.maximum(jnp.max(jnp.abs(values), axis=1), 1e-30)
    codes = jnp.round(values * (LEVELS / top)[:, None, :])
    return codes.astype(jnp.int32).astype(jnp.int16), top * (1.0 / LEVELS)


def decode(codes, unit):
    return codes.astype(jnp.int32).astype(jnp.float32) * unit[:, None, :]


def exchange(
    reps, chips, cap, scale, fused,
    rows_ref, cols_ref, list_ref, chain_ref, tokens_ref, grad_ref, weight_ref,
    result_ref, owned_ref,
    tok, grad, pair_out, pair_in, mine, chip_out, chip_in, chip_unit_out, chip_unit_in,
    padded, codes, units, rep_out, rep_in, rep_unit_out, rep_unit_in,
    load_sem, w_send, w_recv, fw_send, fw_recv, p_send, p_recv, c_send, c_recv, r_send, r_recv,
    cu_send, cu_recv, ru_send, ru_recv,
    *inside,
):
    gathered_ref = inside[0] if fused else result_ref
    rep = lax.axis_index("rep")
    shard = lax.axis_index("fsdp")
    chip, core = shard // 2, shard % 2
    other = chip * 2 + 1 - core
    per, size = weight_ref.shape[0], weight_ref.shape[1]

    def load(source, target, sem):
        def step(b, carry):
            place = pl.ds(pl.multiple_of(b * size, size), size)
            pltpu.make_async_copy(source.at[:, place], target.at[b], sem).start()
            return carry

        lax.fori_loop(0, target.shape[0], step, 0, unroll=8)

    load(tokens_ref, tok, load_sem.at[0])
    load(grad_ref, grad, load_sem.at[1])
    own_slot = gathered_ref.at[pl.ds(shard * per, per)]
    keep = pltpu.make_async_copy(weight_ref, own_slot, load_sem.at[2])
    keep.start()

    def at(d):
        return lax.rem(chip + d, chips)

    def back(d):
        return lax.rem(chip + chips - d, chips)

    barrier = pltpu.get_barrier_semaphore()
    pl.semaphore_signal(barrier, inc=1, device_id=(rep, other), device_id_type=MESH)
    for d in range(1, chips):
        pl.semaphore_signal(
            barrier, inc=1, device_id=(rep, at(d) * 2 + core), device_id_type=MESH
        )
    for d in range(1, reps):
        pl.semaphore_signal(
            barrier, inc=1, device_id=(lax.rem(rep + d, reps), shard), device_id_type=MESH
        )
    pl.semaphore_wait(barrier, chips + reps - 1)

    sends = []

    def remote(src, dst, send, recv, device):
        copy = pltpu.make_async_remote_copy(
            src_ref=src, dst_ref=dst, send_sem=send, recv_sem=recv,
            device_id=device, device_id_type=MESH,
        )
        copy.start()
        sends.append(copy)
        return copy

    forwards = [remote(weight_ref, own_slot, fw_send.at[0], fw_recv.at[0], (rep, other))]
    arrivals = [None]
    for d in range(1, chips):
        arrivals.append(
            remote(weight_ref, own_slot, w_send.at[d], w_recv.at[d], (rep, at(d) * 2 + core))
        )

    pltpu.make_async_copy(tok, tok, load_sem.at[0]).wait()
    pltpu.make_async_copy(grad, grad, load_sem.at[1]).wait()

    def products(first, target):
        def step(j, carry):
            target[j] = lax.dot_general(
                tok[rows_ref[first + j]], grad[cols_ref[first + j]],
                (((0,), (0,)), ((), ())), preferred_element_type=jnp.float32,
            )
            return carry

        lax.fori_loop(0, per, step, 0, unroll=True)

    order = list(range(1, chips)) + [0]
    pairs, chip_copies = {}, {}

    def finish(d):
        pairs[d].wait_recv()
        mine[d] = mine[d] + pair_in[d]
        if d:
            device = (rep, at(d) * 2 + core)
            chip_out[d], chip_unit_out[d] = encode(mine[d])
            chip_copies[d] = (
                remote(chip_unit_out.at[d], chip_unit_in.at[d], cu_send.at[d], cu_recv.at[d], device),
                remote(chip_out.at[d], chip_in.at[d], c_send.at[d], c_recv.at[d], device),
            )

    for n, d in enumerate(order):
        products((at(d) * 2 + 1 - core) * per, pair_out.at[d])
        pairs[d] = remote(
            pair_out.at[d], pair_in.at[d], p_send.at[d], p_recv.at[d], (rep, other)
        )
        products((at(d) * 2 + core) * per, mine.at[d])
        if n:
            finish(order[n - 1])
    finish(0)

    for d in range(1, chips):
        arrivals[d].wait_recv()
        slot = gathered_ref.at[pl.ds((back(d) * 2 + core) * per, per)]
        forwards.append(
            remote(slot, slot, fw_send.at[d], fw_recv.at[d], (rep, other))
        )

    total = mine[0]
    for d in range(1, chips):
        for copy in chip_copies[d]:
            copy.wait_recv()
        total = total + decode(chip_in[d], chip_unit_in[d])
    total = total * scale
    padded[:per] = total
    padded[per] = jnp.zeros((size, size), jnp.float32)
    codes[:per], units[:per] = encode(total)
    codes[per] = jnp.zeros((size, size), jnp.int16)
    units[per:] = jnp.zeros((units.shape[0] - per, size), jnp.float32)

    rep_copies = {}
    for d in range(1, reps):
        peer = lax.rem(rep + d, reps)
        for s in range(cap):
            rep_out[d, s] = codes[list_ref[s, 0, peer]]
            rep_unit_out[d, s] = units[list_ref[s, 0, peer]]
        device = (peer, shard)
        rep_copies[d] = (
            remote(rep_unit_out.at[d], rep_unit_in.at[d], ru_send.at[d], ru_recv.at[d], device),
            remote(rep_out.at[d], rep_in.at[d], r_send.at[d], r_recv.at[d], device),
        )
    if fused:
        _, running = inside
        out = result_ref
        count = running.shape[0] - 1
        running[count] = jnp.zeros(running.shape[1:], jnp.float32)
        for copy in forwards:
            copy.wait_recv()
        keep.wait()

        def chained(k, carry):
            running[k] = running[chain_ref[k]] + lax.dot_general(
                grad[cols_ref[k]], gathered_ref[k],
                (((1,), (1,)), ((), ())), preferred_element_type=jnp.float32,
            )
            return carry

        lax.fori_loop(0, count, chained, 0, unroll=8)
        for r in range(out.shape[1] // size):
            out[:, r * size : (r + 1) * size] = running[chain_ref[count + r]].astype(out.dtype)

    for s in range(cap):
        owned_ref[s] = padded[list_ref[s, 0, rep]]
    for d in range(1, reps):
        for copy in rep_copies[d]:
            copy.wait_recv()
        owned_ref[...] = owned_ref[...] + decode(rep_in[d], rep_unit_in[d])
    for copy in sends:
        copy.wait_send()
    if not fused:
        for copy in forwards:
            copy.wait_recv()
        keep.wait()


def token_kernel(count, rows_ref, cols_ref, grad_ref, weight_ref, out_ref, total):
    size = weight_ref.shape[1]
    total[...] = jnp.zeros_like(total)

    def step(k, carry):
        col = pl.multiple_of(cols_ref[k] * size, size)
        row = rows_ref[k]
        total[row] = total[row] + lax.dot_general(
            grad_ref[:, pl.ds(col, size)], weight_ref[k],
            (((1,), (1,)), ((), ())), preferred_element_type=jnp.float32,
        )
        return carry

    lax.fori_loop(0, count, step, 0, unroll=8)
    for r in range(total.shape[0]):
        out_ref[:, r * size : (r + 1) * size] = total[r].astype(out_ref.dtype)


def local(tokens, out_grad, weight_blocks, block_row, block_col, send_list):
    rows_here, width = tokens.shape
    wide = out_grad.shape[1]
    per, size = weight_blocks.shape[:2]
    reps, shards = lax.axis_size("rep"), lax.axis_size("fsdp")
    chips, cap = shards // 2, send_list.shape[2]
    count = shards * per
    scale = float(rows_here * reps * shards) ** (-0.5)
    smem = pl.BlockSpec(memory_space=pltpu.SMEM)
    vmem = pl.BlockSpec(memory_space=pltpu.VMEM)
    hbm = pl.BlockSpec(memory_space=pl.ANY)
    f32 = jnp.float32
    dma = pltpu.SemaphoreType.DMA
    gathered_shape = (count, size, size)
    inside, fused = [], count * rows_here * size * 4 <= 12 * 2**20
    chain = block_row
    result_shape = jax.ShapeDtypeStruct(gathered_shape, weight_blocks.dtype)
    if fused:
        row_total = width // size
        result_shape = pltpu.VMEM((rows_here, width), jnp.bfloat16)
        inside = [
            pltpu.VMEM(gathered_shape, weight_blocks.dtype),
            pltpu.VMEM((count + 1, rows_here, size), f32),
        ]
        serial = jnp.arange(count, dtype=jnp.int32)
        keys = jnp.concatenate([block_row, jnp.arange(row_total, dtype=jnp.int32)])
        ends = jnp.minimum(jnp.arange(count + row_total, dtype=jnp.int32), count)
        found = (keys[:, None] == block_row[None, :]) & (serial[None, :] < ends[:, None])
        latest = jnp.max(jnp.where(found, serial[None, :], -1), axis=1)
        chain = jnp.where(latest < 0, count, latest)
    result, owned = pl.pallas_call(
        functools.partial(exchange, reps, chips, cap, scale, fused),
        out_shape=(
            result_shape,
            jax.ShapeDtypeStruct((cap, size, size), f32),
        ),
        in_specs=[smem, smem, smem, smem, hbm, hbm, hbm],
        out_specs=(vmem if fused else hbm, vmem),
        scratch_shapes=[
            pltpu.VMEM((width // size, rows_here, size), tokens.dtype),
            pltpu.VMEM((wide // size, rows_here, size), out_grad.dtype),
            pltpu.VMEM((chips, per, size, size), f32),
            pltpu.VMEM((chips, per, size, size), f32),
            pltpu.VMEM((chips, per, size, size), f32),
            pltpu.VMEM((chips, per, size, size), jnp.int16),
            pltpu.VMEM((chips, per, size, size), jnp.int16),
            pltpu.VMEM((chips, per, size), f32),
            pltpu.VMEM((chips, per, size), f32),
            pltpu.VMEM((per + 1, size, size), f32),
            pltpu.VMEM((per + 1, size, size), jnp.int16),
            pltpu.VMEM((per + 8, size), f32),
            pltpu.VMEM((reps, cap, size, size), jnp.int16),
            pltpu.VMEM((reps, cap, size, size), jnp.int16),
            pltpu.VMEM((reps, cap, size), f32),
            pltpu.VMEM((reps, cap, size), f32),
            dma((3,)), dma((chips,)), dma((chips,)), dma((chips,)), dma((chips,)),
            dma((chips,)), dma((chips,)), dma((chips,)), dma((chips,)),
            dma((reps,)), dma((reps,)),
            dma((chips,)), dma((chips,)), dma((reps,)), dma((reps,)),
            *inside,
        ],
        compiler_params=pltpu.CompilerParams(
            collective_id=0, has_side_effects=True, vmem_limit_bytes=56 * 2**20
        ),
    )(block_row, block_col, jnp.transpose(send_list, (2, 0, 1)), chain, tokens, out_grad, weight_blocks)
    if fused:
        return (result, owned[None, None])
    token_grad = pl.pallas_call(
        functools.partial(token_kernel, count),
        out_shape=jax.ShapeDtypeStruct((rows_here, width), jnp.bfloat16),
        in_specs=[smem, smem, vmem, vmem],
        out_specs=vmem,
        scratch_shapes=[pltpu.VMEM((width // size, rows_here, size), f32)],
        compiler_params=pltpu.CompilerParams(vmem_limit_bytes=48 * 2**20),
    )(block_row, block_col, out_grad, result)
    return (token_grad, owned[None, None])


def solution(mesh):
    return jax.shard_map(
        local,
        mesh=mesh,
        in_specs=(
            P(("rep", "fsdp"), None),
            P(("rep", "fsdp"), None),
            P("fsdp", None, None),
            P(),
            P(),
            P("fsdp", None, None),
        ),
        out_specs=(P(("rep", "fsdp"), None), P("rep", "fsdp", None, None, None)),
        check_vma=False,
    )
```
